32 devices in a mesh: clip: 16 (over z, y, core), row: 2 (over x).
Axes of the slice: x: 2, y: 2, z: 4, core: 2. Of those that a mesh axis runs over, the one named last changes fastest.
Arguments:
- video: bfloat16 [64, 16, 320, 128], P('clip', 'row'), may hold values from -6 to 6
- spatial_one: bfloat16 [3, 3, 320, 320], replicated, may hold values from -0.109375 to 0.109375
- spatial_two: bfloat16 [3, 3, 320, 320], replicated, may hold values from -0.109375 to 0.109375
- temporal_mix: bfloat16 [3, 320, 320], replicated, may hold values from -0.1875 to 0.1875
- bias_one: float32 [320], replicated, may hold values from -3 to 3
- bias_two: float32 [320], replicated, may hold values from -3 to 3
- bias_three: float32 [320], replicated, may hold values from -3 to 3
Outputs:
- block_out: bfloat16 [64, 16, 320, 128], P('clip', 'row')
The draws below stay inside these ranges and needn't reach their ends.
All inputs are finite; a program needn't handle non-finite values.
Results may differ from the reference program's by a relative error of at most 0.011.
Values may be sent and summed in bfloat16 or wider, within the bound.
A program may use at most 128 MiB of HBM per device.

```python
import jax
import jax.numpy as jnp
from jax import lax

C = 320
W = 128
FRAMES = 64
HEIGHT = 16


def steps_of(key, extent, shards, low, top_value):
    gain, own = 1.0, jax.random.fold_in(key, 6)
    for dim, shards_of in shards:
        steps = jnp.exp(jax.random.uniform(jax.random.fold_in(own, dim), (shards_of,), jnp.float32, low / len(shards), top_value / len(shards)))
        gain = gain * jnp.repeat(steps, extent[dim] // shards_of).reshape([-1 if axis == dim else 1 for axis in range(len(extent))])
    return gain


def gaussian(key, shape, deviation, reach, cuts=(), kind=jnp.bfloat16):
    level = steps_of(key, shape, cuts, -0.22, 0.18) if cuts else 1.0
    values = jax.random.normal(key, shape, jnp.float32) * deviation * level
    return jnp.minimum(jnp.maximum(values, -reach), reach).astype(kind)


def setup_inputs(seed: int = 0) -> dict:
    keys = jax.random.split(jax.random.key(seed), 8)
    video = gaussian(keys[0], (FRAMES, HEIGHT, C, W), 1.0, 6.0, ((0, 16), (1, 2)))
    spatial_one = gaussian(keys[1], (3, 3, C, C), (9 * C) ** -0.5, 0.109375)
    spatial_two = gaussian(keys[2], (3, 3, C, C), (9 * C) ** -0.5, 0.109375)
    temporal_mix = gaussian(keys[3], (3, C, C), (3 * C) ** -0.5, 0.1875)
    bias_one = gaussian(keys[4], (C,), 0.5, 3.0, (), jnp.float32)
    bias_two = gaussian(keys[5], (C,), 0.5, 3.0, (), jnp.float32)
    bias_three = gaussian(keys[6], (C,), 0.5, 3.0, (), jnp.float32)
    return dict(video=video, spatial_one=spatial_one, spatial_two=spatial_two, temporal_mix=temporal_mix, bias_one=bias_one, bias_two=bias_two, bias_three=bias_three)


def silu_round(values):
    return jax.nn.silu(values.astype(jnp.float32)).astype(jnp.bfloat16)


def conv_frame(activated, kernel):
    height = activated.shape[0]
    width = activated.shape[2]
    padded = jnp.pad(activated, ((1, 1), (0, 0), (1, 1)))
    total = jnp.zeros((height, kernel.shape[2], width), jnp.float32)
    for row_tap in range(3):
        for column_tap in range(3):
            window = padded[row_tap:row_tap + height, :, column_tap:column_tap + width]
            total = total + jnp.einsum('oc,hcw->how', kernel[row_tap, column_tap].astype(jnp.float32), window.astype(jnp.float32))
    return total


def spatial_frame(frame, kernel, bias_vec):
    activated = silu_round(frame)
    return (frame.astype(jnp.float32) + bias_vec[:, None] + conv_frame(activated, kernel)).astype(jnp.bfloat16)


def reference(video, spatial_one, spatial_two, temporal_mix, bias_one, bias_two, bias_three):
    first_out = lax.map(lambda frame: spatial_frame(frame, spatial_one, bias_one), video)
    second_out = lax.map(lambda frame: spatial_frame(frame, spatial_two, bias_two), first_out)
    act_three = lax.map(silu_round, second_out)
    padded = jnp.pad(act_three, ((1, 1), (0, 0), (0, 0), (0, 0)))
    mix_weight = temporal_mix.astype(jnp.float32)

    def temporal_frame(frame_index):
        window = lax.dynamic_slice_in_dim(padded, frame_index, 3, 0)
        centre = lax.dynamic_index_in_dim(second_out, frame_index, 0, keepdims=False)
        total = jnp.einsum('koc,khcw->how', mix_weight, window.astype(jnp.float32))
        return (centre.astype(jnp.float32) + bias_three[:, None] + total).astype(jnp.bfloat16)

    return lax.map(temporal_frame, jnp.arange(video.shape[0], dtype=jnp.int32))
```

```python
import functools

import jax
import jax.numpy as jnp
from jax import lax
from jax.experimental import pallas as pl
from jax.experimental.pallas import tpu as pltpu
from jax.sharding import PartitionSpec as P

BF16, F32 = jnp.bfloat16, jnp.float32
MESH = pl.DeviceIdType.MESH
PARTS = 2


def silu(v):
    half = 0.5 * v
    return half + half * jnp.tanh(half)


def kernel(
    clips, bands, video, w_one, w_two, w_mix, b_one, b_two, b_three, out,
    raw_one, raw_two, raw_mix, mat_one, mat_two, mat_mix, cols, x, act_one, act_two, act_three,
    w_sem, x_sem, o_sem, row_send, row_recv, clip_send, clip_recv,
):
    frames, half, c, wide = x.shape
    w = wide // 2
    n = c // PARTS
    clip, band = lax.axis_index("clip"), lax.axis_index("row")
    has_up, has_down = band > 0, band < bands - 1
    has_prev, has_next = clip > 0, clip < clips - 1
    first = jnp.where(lax.rem(clip, 2) == 0, 0, frames - 1)
    order = [first, frames - 1 - first] + list(range(1, frames - 1))

    loads_one = [pltpu.make_async_copy(w_one.at[:, j], raw_one.at[:, j], w_sem.at[j]) for j in range(3)]
    load_two = pltpu.make_async_copy(w_two, raw_two, w_sem.at[3])
    load_mix = pltpu.make_async_copy(w_mix, raw_mix, w_sem.at[4])

    def load_x(f):
        return [
            pltpu.make_async_copy(
                video.at[f, pl.ds(k * half, half)], x.at[f, :, :, pl.ds(k * w, w)], x_sem.at[f, k])
            for k in range(2)
        ]

    def start_all(copies):
        for copy in copies:
            copy.start()

    start_all(load_x(order[0]))
    start_all(loads_one)
    for f in order[1:]:
        start_all(load_x(f))
    load_two.start()
    load_mix.start()

    barrier = pltpu.get_barrier_semaphore()
    neighbours = (
        (has_up, {"row": band - 1}), (has_down, {"row": band + 1}),
        (has_prev, {"clip": clip - 1}), (has_next, {"clip": clip + 1}),
    )

    def where_to(place):
        return (place.get("clip", clip), place.get("row", band))

    for there, place in neighbours:
        @pl.when(there)
        def _():
            pl.semaphore_signal(barrier, inc=1, device_id=where_to(place), device_id_type=MESH)
    pl.semaphore_wait(barrier, sum(there.astype(jnp.int32) for there, _place in neighbours))

    for k, bias in enumerate((b_one, b_two, b_three)):
        eye = lax.broadcasted_iota(jnp.int32, (c, c), 0) == lax.broadcasted_iota(jnp.int32, (c, c), 1)
        column = jnp.sum(jnp.where(eye, bias[...], 0.0), axis=1, keepdims=True)
        cols[k] = jnp.broadcast_to(column, (c, w))

    lo, hi = pl.ds(0, w), pl.ds(w, w)

    def slot(t):
        return pl.ds(t * c, c)

    def row_copies(act, stage, f):
        up = pltpu.make_async_remote_copy(
            src_ref=act.at[f, slot(1), lo], dst_ref=act.at[f, slot(half + 1), hi],
            send_sem=row_send.at[stage, f, 0], recv_sem=row_recv.at[stage, f, 0],
            device_id=(clip, band - 1), device_id_type=MESH)
        down = pltpu.make_async_remote_copy(
            src_ref=act.at[f, slot(half), hi], dst_ref=act.at[f, slot(0), lo],
            send_sem=row_send.at[stage, f, 1], recv_sem=row_recv.at[stage, f, 1],
            device_id=(clip, band + 1), device_id_type=MESH)
        return up, down

    def send_rows(act, stage, f):
        up, down = row_copies(act, stage, f)
        pl.when(has_up)(up.start)
        pl.when(has_down)(down.start)

        @pl.when(jnp.logical_not(has_up))
        def _():
            act[f, slot(0), lo] = jnp.zeros((c, w), BF16)

        @pl.when(jnp.logical_not(has_down))
        def _():
            act[f, slot(half + 1), hi] = jnp.zeros((c, w), BF16)

        act[f, slot(half + 1), lo] = act[f, slot(1), hi]
        act[f, slot(0), hi] = act[f, slot(half), lo]

    def clip_copies(s):
        back = pltpu.make_async_remote_copy(
            src_ref=act_three.at[s, slot(1)], dst_ref=act_three.at[s, slot(frames + 1)],
            send_sem=clip_send.at[0, s], recv_sem=clip_recv.at[0, s],
            device_id=(clip - 1, band), device_id_type=MESH)
        ahead = pltpu.make_async_remote_copy(
            src_ref=act_three.at[s, slot(frames)], dst_ref=act_three.at[s, slot(0)],
            send_sem=clip_send.at[1, s], recv_sem=clip_recv.at[1, s],
            device_id=(clip + 1, band), device_id_type=MESH)
        return back, ahead

    def activate(f, s):
        act_one[f, pl.ds(pl.multiple_of((s + 1) * c, c), c), :] = silu(x[f, s].astype(F32)).astype(BF16)

    lane = lax.broadcasted_iota(jnp.int32, (n, w), 1)
    not_first, not_last = lane > 0, lane < w - 1

    def conv_slab(mat, act, stage, f, s):
        window = act[f, pl.ds(pl.multiple_of(s * c, c), 3 * c), :]
        for part in range(PARTS):
            rows = pl.ds(part * n, n)
            product = jnp.dot(mat[part], window, preferred_element_type=F32)
            bias = cols[stage, rows, :]
            for k in range(2):
                lanes = pl.ds(k * w, w)
                cut = slice(k * w, (k + 1) * w)
                left = jnp.where(not_first, pltpu.roll(product[:n, cut], 1, 1), 0.0)
                right = jnp.where(not_last, pltpu.roll(product[2 * n:, cut], w - 1, 1), 0.0)
                total = x[f, s, rows, lanes].astype(F32) + bias + (left + product[n:2 * n, cut] + right)
                rounded = total.astype(BF16)
                x[f, s, rows, lanes] = rounded
                active = silu(rounded.astype(F32)).astype(BF16)
                if stage == 0:
                    act_two[f, pl.ds(pl.multiple_of((s + 1) * c + part * n, 16), n), lanes] = active
                else:
                    act_three[s, pl.ds(pl.multiple_of((f + 1) * c + part * n, 16), n), lanes] = active

    def conv(stage, f, other=None):
        mat, act = (mat_one, act_one) if stage == 0 else (mat_two, act_two)

        def step(i, carry):
            @pl.when(i == half - 2)
            def _():
                up, down = row_copies(act, stage, f)
                pl.when(has_down)(up.wait_recv)
                pl.when(has_up)(down.wait_recv)

            s = jnp.where(i < half - 2, i + 1, jnp.where(i == half - 2, 0, half - 1))
            if other is not None:
                activate(other, i)
            conv_slab(mat, act, stage, f, s)
            if stage == 1:
                back, ahead = clip_copies(s)
                pl.when(jnp.logical_and(f == 0, has_prev))(back.start)
                pl.when(jnp.logical_and(f == frames - 1, has_next))(ahead.start)
            return carry

        if other is not None:
            for copy in load_x(other):
                copy.wait()
        lax.fori_loop(0, half, step, 0)
        if other is not None:
            send_rows(act_one, 0, other)
        if stage == 0:
            send_rows(act_two, 1, f)

    for copy in load_x(order[0]):
        copy.wait()

    def first_step(s, carry):
        activate(order[0], s)
        return carry

    lax.fori_loop(0, half, first_step, 0)
    send_rows(act_one, 0, order[0])

    def pack(raw, mat):
        for part in range(PARTS):
            for j in range(3):
                mat[part, pl.ds(j * n, n), :] = jnp.concatenate(
                    [raw[i, j, pl.ds(part * n, n), :] for i in range(3)], axis=1)

    for copy in loads_one:
        copy.wait()
    pack(raw_one, mat_one)

    conv(0, order[0], order[1])
    load_two.wait()
    pack(raw_two, mat_two)
    load_mix.wait()
    mat_mix[...] = jnp.concatenate([raw_mix[k] for k in range(3)], axis=1)

    for k, f in enumerate(order):
        if k + 1 < frames:
            conv(0, order[k + 1], order[k + 2] if k + 2 < frames else None)
        conv(1, f)

    @pl.when(jnp.logical_not(has_prev))
    def _():
        act_three[:, slot(0), :] = jnp.zeros((half, c, wide), BF16)

    @pl.when(jnp.logical_not(has_next))
    def _():
        act_three[:, slot(frames + 1), :] = jnp.zeros((half, c, wide), BF16)

    def out_copies(f, s):
        return [
            pltpu.make_async_copy(
                x.at[f, s, :, pl.ds(k * w, w)], out.at[f, s + k * half], o_sem.at[f, s, k])
            for k in range(2)
        ]

    def temporal(f, waits):
        def step(s, carry):
            back, ahead = clip_copies(s)
            if waits:
                pl.when(jnp.logical_and(f == frames - 1, has_next))(back.wait_recv)
                pl.when(jnp.logical_and(f == 0, has_prev))(ahead.wait_recv)
            window = act_three[s, pl.ds(pl.multiple_of(f * c, c), 3 * c), :]
            product = jnp.dot(mat_mix[...], window, preferred_element_type=F32)
            for k in range(2):
                lanes = pl.ds(k * w, w)
                total = x[f, s, :, lanes].astype(F32) + cols[2] + product[:, k * w:(k + 1) * w]
                x[f, s, :, lanes] = total.astype(BF16)
            start_all(out_copies(f, s))
            return carry

        lax.fori_loop(0, half, step, 0)

    for f in order[2:]:
        temporal(f, False)
    temporal(order[1], True)
    temporal(order[0], True)

    def finish(s, carry):
        for f in range(frames):
            for copy in out_copies(f, s):
                copy.wait()
        back, ahead = clip_copies(s)
        pl.when(has_prev)(back.wait_send)
        pl.when(has_next)(ahead.wait_send)
        return carry

    lax.fori_loop(0, half, finish, 0)
    for stage, act in ((0, act_one), (1, act_two)):
        for f in range(frames):
            up, down = row_copies(act, stage, f)
            pl.when(has_up)(up.wait_send)
            pl.when(has_down)(down.wait_send)


def body(clips, bands, video, spatial_one, spatial_two, temporal_mix, bias_one, bias_two, bias_three):
    frames, rows, c, w = video.shape
    half = rows // 2
    anywhere = pl.BlockSpec(memory_space=pl.ANY)
    vmem = pl.BlockSpec(memory_space=pltpu.VMEM)
    act = pltpu.VMEM((frames, (half + 2) * c, 2 * w), BF16)
    flops = 2 * frames * rows * w * c * c * 21
    return pl.pallas_call(
        functools.partial(kernel, clips, bands),
        out_shape=jax.ShapeDtypeStruct(video.shape, BF16),
        in_specs=[anywhere] * 4 + [vmem] * 3,
        out_specs=anywhere,
        scratch_shapes=[
            pltpu.VMEM(spatial_one.shape, BF16),
            pltpu.VMEM(spatial_two.shape, BF16),
            pltpu.VMEM(temporal_mix.shape, BF16),
            pltpu.VMEM((PARTS, 3 * c // PARTS, 3 * c), BF16),
            pltpu.VMEM((PARTS, 3 * c // PARTS, 3 * c), BF16),
            pltpu.VMEM((c, 3 * c), BF16),
            pltpu.VMEM((3, c, w), F32),
            pltpu.VMEM((frames, half, c, 2 * w), BF16),
            act,
            act,
            pltpu.VMEM((half, (frames + 2) * c, 2 * w), BF16),
            pltpu.SemaphoreType.DMA((5,)),
            pltpu.SemaphoreType.DMA((frames, 2)),
            pltpu.SemaphoreType.DMA((frames, half, 2)),
            pltpu.SemaphoreType.DMA((2, frames, 2)),
            pltpu.SemaphoreType.DMA((2, frames, 2)),
            pltpu.SemaphoreType.DMA((2, half)),
            pltpu.SemaphoreType.DMA((2, half)),
        ],
        cost_estimate=pl.CostEstimate(flops=flops, bytes_accessed=4 * video.size, transcendentals=0),
        compiler_params=pltpu.CompilerParams(
            collective_id=0, has_side_effects=True, vmem_limit_bytes=62 * 2**20),
    )(
        video, spatial_one, spatial_two, temporal_mix,
        bias_one.reshape(1, c), bias_two.reshape(1, c), bias_three.reshape(1, c),
    )


def solution(mesh):
    placed = (P("clip", "row", None, None), P(), P(), P(), P(), P(), P())
    return jax.shard_map(
        functools.partial(body, mesh.shape["clip"], mesh.shape["row"]),
        mesh=mesh, in_specs=placed, out_specs=P("clip", "row", None, None), check_vma=False,
    )
```

```python
import functools

import jax
import jax.numpy as jnp
from jax import lax
from jax.experimental import pallas as pl
from jax.experimental.pallas import tpu as pltpu
from jax.sharding import PartitionSpec as P

BF16, F32 = jnp.bfloat16, jnp.float32
MESH = pl.DeviceIdType.MESH
CHUNK = 64


def silu(v):
    half = 0.5 * v
    return half + half * jnp.tanh(half)


def kernel(
    clips, bands, video, w_one, w_two, w_mix, b_one, b_two, b_three, out,
    raw_one, raw_two, raw_mix, mat_one, mat_two, mat_mix, cols, x, act_one, act_two, act_three, prod_a, prod_b,
    w_sem, x_sem, o_sem, row_send, row_recv, clip_send, clip_recv,
):
    frames, half, c, wide = x.shape
    w = wide // 2
    n = CHUNK
    clip, band = lax.axis_index("clip"), lax.axis_index("row")
    has_up, has_down = band > 0, band < bands - 1
    has_prev, has_next = clip > 0, clip < clips - 1
    first = jnp.where(lax.rem(clip, 2) == 0, 0, frames - 1)
    order = [first, frames - 1 - first] + list(range(1, frames - 1))

    loads_one = [pltpu.make_async_copy(w_one.at[:, j], raw_one.at[:, j], w_sem.at[j]) for j in range(3)]
    load_two = pltpu.make_async_copy(w_two, raw_two, w_sem.at[3])
    load_mix = pltpu.make_async_copy(w_mix, raw_mix, w_sem.at[4])

    def load_x(f):
        return [
            pltpu.make_async_copy(
                video.at[f, pl.ds(k * half, half)], x.at[f, :, :, pl.ds(k * w, w)], x_sem.at[f, k])
            for k in range(2)
        ]

    def start_all(copies):
        for copy in copies:
            copy.start()

    start_all(load_x(order[0]))
    start_all(loads_one)
    for f in order[1:]:
        start_all(load_x(f))
    load_two.start()
    load_mix.start()

    barrier = pltpu.get_barrier_semaphore()
    neighbours = (
        (has_up, {"row": band - 1}), (has_down, {"row": band + 1}),
        (has_prev, {"clip": clip - 1}), (has_next, {"clip": clip + 1}),
    )

    def where_to(place):
        return (place.get("clip", clip), place.get("row", band))

    for there, place in neighbours:
        @pl.when(there)
        def _():
            pl.semaphore_signal(barrier, inc=1, device_id=where_to(place), device_id_type=MESH)
    pl.semaphore_wait(barrier, sum(there.astype(jnp.int32) for there, _place in neighbours))

    for k, bias in enumerate((b_one, b_two, b_three)):
        eye = lax.broadcasted_iota(jnp.int32, (c, c), 0) == lax.broadcasted_iota(jnp.int32, (c, c), 1)
        column = jnp.sum(jnp.where(eye, bias[...][None, :], 0.0), axis=1, keepdims=True)
        cols[k] = jnp.broadcast_to(column, (c, w))

    lo, hi = pl.ds(0, w), pl.ds(w, w)

    def slot(t):
        return pl.ds(t * c, c)

    def row_copies(act, stage, f):
        up = pltpu.make_async_remote_copy(
            src_ref=act.at[f, slot(1), lo], dst_ref=act.at[f, slot(half + 1), hi],
            send_sem=row_send.at[stage, f, 0], recv_sem=row_recv.at[stage, f, 0],
            device_id=(clip, band - 1), device_id_type=MESH)
        down = pltpu.make_async_remote_copy(
            src_ref=act.at[f, slot(half), hi], dst_ref=act.at[f, slot(0), lo],
            send_sem=row_send.at[stage, f, 1], recv_sem=row_recv.at[stage, f, 1],
            device_id=(clip, band + 1), device_id_type=MESH)
        return up, down

    def send_rows(act, stage, f):
        up, down = row_copies(act, stage, f)
        pl.when(has_up)(up.start)
        pl.when(has_down)(down.start)

        @pl.when(jnp.logical_not(has_up))
        def _():
            act[f, slot(0), lo] = jnp.zeros((c, w), BF16)

        @pl.when(jnp.logical_not(has_down))
        def _():
            act[f, slot(half + 1), hi] = jnp.zeros((c, w), BF16)

        act[f, slot(half + 1), lo] = act[f, slot(1), hi]
        act[f, slot(0), hi] = act[f, slot(half), lo]

    def clip_copies(s):
        back = pltpu.make_async_remote_copy(
            src_ref=act_three.at[s, slot(1)], dst_ref=act_three.at[s, slot(frames + 1)],
            send_sem=clip_send.at[0, s], recv_sem=clip_recv.at[0, s],
            device_id=(clip - 1, band), device_id_type=MESH)
        ahead = pltpu.make_async_remote_copy(
            src_ref=act_three.at[s, slot(frames)], dst_ref=act_three.at[s, slot(0)],
            send_sem=clip_send.at[1, s], recv_sem=clip_recv.at[1, s],
            device_id=(clip + 1, band), device_id_type=MESH)
        return back, ahead

    def activate(f, s):
        act_one[f, pl.ds(pl.multiple_of((s + 1) * c, c), c), :] = silu(x[f, s].astype(F32)).astype(BF16)

    lane = lax.broadcasted_iota(jnp.int32, (n, w), 1)
    not_first, not_last = lane > 0, lane < w - 1

    def multiply(stage, f, s, product):
        mat, act = ((mat_one, act_one), (mat_two, act_two))[stage]
        window = act[f, pl.ds(s * c, 3 * c), :]
        product[...] = jnp.dot(mat[...], window, preferred_element_type=F32)

    def finish_slab(stage, f, s, product):
        for part in range(c // n):
            rows = pl.ds(part * n, n)
            bias = cols[stage, rows, :]
            for lanes in (lo, hi):
                left = jnp.where(not_first, pltpu.roll(product[rows, lanes], 1, 1), 0.0)
                right = jnp.where(not_last, pltpu.roll(product[pl.ds(2 * c + part * n, n), lanes], w - 1, 1), 0.0)
                middle = product[pl.ds(c + part * n, n), lanes]
                total = x[f, s, rows, lanes].astype(F32) + bias + (left + middle + right)
                rounded = total.astype(BF16)
                x[f, s, rows, lanes] = rounded
                active = silu(rounded.astype(F32)).astype(BF16)
                if stage == 0:
                    act_two[f, pl.ds((s + 1) * c + part * n, n), lanes] = active
                else:
                    act_three[s, pl.ds(pl.multiple_of((f + 1) * c + part * n, 16), n), lanes] = active
        if stage == 1:
            back, ahead = clip_copies(s)
            pl.when(jnp.logical_and(f == 0, has_prev))(back.start)
            pl.when(jnp.logical_and(f == frames - 1, has_next))(ahead.start)

    products = (prod_a, prod_b)
    row_order = list(range(1, half - 1)) + [0, half - 1]

    def conv(stage, f, pending, other=None):
        act = act_one if stage == 0 else act_two
        if other is not None:
            for copy in load_x(other):
                copy.wait()
        for i, s in enumerate(row_order):
            if i == half - 2:
                up, down = row_copies(act, stage, f)
                pl.when(has_down)(up.wait_recv)
                pl.when(has_up)(down.wait_recv)
            multiply(stage, f, s, products[i % 2])
            if pending is not None:
                finish_slab(*pending)
                if i == 0 and pending[0] == 0:
                    send_rows(act_two, 1, pending[1])
            if other is not None:
                activate(other, i)
            pending = (stage, f, s, products[i % 2])
        if other is not None:
            send_rows(act_one, 0, other)
        return pending

    for copy in load_x(order[0]):
        copy.wait()

    def first_step(s, carry):
        activate(order[0], s)
        return carry

    lax.fori_loop(0, half, first_step, 0)
    send_rows(act_one, 0, order[0])

    def pack(raw, mat):
        for j in range(3):
            mat[pl.ds(j * c, c), :] = jnp.concatenate([raw[i, j] for i in range(3)], axis=1)

    for copy in loads_one:
        copy.wait()
    pack(raw_one, mat_one)

    pending = conv(0, order[0], None, order[1])
    load_two.wait()
    pack(raw_two, mat_two)
    load_mix.wait()
    mat_mix[...] = jnp.concatenate([raw_mix[k] for k in range(3)], axis=1)

    for k, f in enumerate(order):
        if k + 1 < frames:
            pending = conv(0, order[k + 1], pending, order[k + 2] if k + 2 < frames else None)
        elif pending[0] == 0:
            finish_slab(*pending)
            send_rows(act_two, 1, pending[1])
            pending = None
        pending = conv(1, f, pending)
    finish_slab(*pending)

    @pl.when(jnp.logical_not(has_prev))
    def _():
        act_three[:, slot(0), :] = jnp.zeros((half, c, wide), BF16)

    @pl.when(jnp.logical_not(has_next))
    def _():
        act_three[:, slot(frames + 1), :] = jnp.zeros((half, c, wide), BF16)

    def out_copies(f, s):
        return [
            pltpu.make_async_copy(
                x.at[f, s, :, pl.ds(k * w, w)], out.at[f, s + k * half], o_sem.at[f, s, k])
            for k in range(2)
        ]

    def temporal(f, waits):
        def step(s, carry):
            back, ahead = clip_copies(s)
            if waits:
                pl.when(jnp.logical_and(f == frames - 1, has_next))(back.wait_recv)
                pl.when(jnp.logical_and(f == 0, has_prev))(ahead.wait_recv)
            window = act_three[s, pl.ds(pl.multiple_of(f * c, c), 3 * c), :]
            product = jnp.dot(mat_mix[...], window, preferred_element_type=F32)
            for k in range(2):
                lanes = pl.ds(k * w, w)
                total = x[f, s, :, lanes].astype(F32) + cols[2] + product[:, k * w:(k + 1) * w]
                x[f, s, :, lanes] = total.astype(BF16)
            start_all(out_copies(f, s))
            return carry

        lax.fori_loop(0, half, step, 0)

    for f in order[2:]:
        temporal(f, False)
    temporal(order[1], True)
    temporal(order[0], True)

    def finish(s, carry):
        for f in range(frames):
            for copy in out_copies(f, s):
                copy.wait()
        back, ahead = clip_copies(s)
        pl.when(has_prev)(back.wait_send)
        pl.when(has_next)(ahead.wait_send)
        return carry

    lax.fori_loop(0, half, finish, 0)
    for stage, act in ((0, act_one), (1, act_two)):
        for f in range(frames):
            up, down = row_copies(act, stage, f)
            pl.when(has_up)(up.wait_send)
            pl.when(has_down)(down.wait_send)


def body(clips, bands, video, spatial_one, spatial_two, temporal_mix, bias_one, bias_two, bias_three):
    frames, rows, c, w = video.shape
    half = rows // 2
    anywhere = pl.BlockSpec(memory_space=pl.ANY)
    vmem = pl.BlockSpec(memory_space=pltpu.VMEM)
    act = pltpu.VMEM((frames, (half + 2) * c, 2 * w), BF16)
    flops = 2 * frames * rows * w * c * c * 21
    return pl.pallas_call(
        functools.partial(kernel, clips, bands),
        out_shape=jax.ShapeDtypeStruct(video.shape, BF16),
        in_specs=[anywhere] * 4 + [vmem] * 3,
        out_specs=anywhere,
        scratch_shapes=[
            pltpu.VMEM(spatial_one.shape, BF16),
            pltpu.VMEM(spatial_two.shape, BF16),
            pltpu.VMEM(temporal_mix.shape, BF16),
            pltpu.VMEM((3 * c, 3 * c), BF16),
            pltpu.VMEM((3 * c, 3 * c), BF16),
            pltpu.VMEM((c, 3 * c), BF16),
            pltpu.VMEM((3, c, w), F32),
            pltpu.VMEM((frames, half, c, 2 * w), BF16),
            act,
            act,
            pltpu.VMEM((half, (frames + 2) * c, 2 * w), BF16),
            pltpu.VMEM((3 * c, 2 * w), F32),
            pltpu.VMEM((3 * c, 2 * w), F32),
            pltpu.SemaphoreType.DMA((5,)),
            pltpu.SemaphoreType.DMA((frames, 2)),
            pltpu.SemaphoreType.DMA((frames, half, 2)),
            pltpu.SemaphoreType.DMA((2, frames, 2)),
            pltpu.SemaphoreType.DMA((2, frames, 2)),
            pltpu.SemaphoreType.DMA((2, half)),
            pltpu.SemaphoreType.DMA((2, half)),
        ],
        cost_estimate=pl.CostEstimate(flops=flops, bytes_accessed=4 * video.size, transcendentals=0),
        compiler_params=pltpu.CompilerParams(
            collective_id=0, has_side_effects=True, vmem_limit_bytes=62 * 2**20),
    )(
        video, spatial_one, spatial_two, temporal_mix,
        bias_one, bias_two, bias_three,
    )


def solution(mesh):
    placed = (P("clip", "row", None, None), P(), P(), P(), P(), P(), P())
    return jax.shard_map(
        functools.partial(body, mesh.shape["clip"], mesh.shape["row"]),
        mesh=mesh, in_specs=placed, out_specs=P("clip", "row", None, None), check_vma=False,
    )
```
